32 devices in a mesh: panel: 4 (over x, core), front: 8 (over z, y).
Axes of the slice: x: 2, y: 2, z: 4, core: 2. Of those that a mesh axis runs over, the one named last changes fastest.
Arguments:
- rhs: float32 [4, 64, 64, 2, 128], P('panel', None, 'front'), may hold values from -6 to 6
- fronts: bfloat16 [4, 2, 8192, 8192], P('panel', None, 'front'), may hold values from -0.046875 to 0.046875
- wave_sq: float32 [4, 64, 128], P('panel', 'front'), may hold values from 0.5 to 2
- pml_width: int32 [4], P('panel'), may hold values from 1 to 16
Outputs:
- sweep_field: float32 [4, 64, 64, 2, 128], P('panel', None, 'front')
- residual: float32 [4, 64, 64, 2, 128], P('panel', None, 'front')
The draws below stay inside these ranges and needn't reach their ends.
All inputs are finite; a program needn't handle non-finite values.
Results may differ from the reference program's by a relative error of at most 0.013.
Values may be sent and summed in bfloat16 or wider, within the bound.
No kernel may reach another device: no remote copies, remote signals or barrier semaphores. Data moves between devices by JAX's collectives and lax.ppermute only.
A program may use at most 64 MiB of HBM per device.

```python
import jax
import jax.numpy as jnp

NRHS = 64
PX = 64
PY = 128
CF = 8192
FRONT = 16384
NQ = 4


def place_ends(array, key, least, top_value):
    index_at = [jax.random.randint(jax.random.fold_in(key, axis), (), 0, length) for axis, length in enumerate(array.shape)]
    widest = array.shape.index(max(array.shape))
    beside = index_at[:widest] + [(index_at[widest] + 1) % array.shape[widest]] + index_at[widest + 1:]
    return array.at[tuple(index_at)].set(least).at[tuple(beside)].set(top_value)


def block_levels(key, shape, pieces, low, top_value):
    def one(position, parts):
        draws = jax.random.uniform(jax.random.fold_in(jax.random.fold_in(key, 6), position), (parts,), jnp.float32, low / len(pieces), top_value / len(pieces))
        return jnp.repeat(jnp.exp(draws), shape[position] // parts).reshape((-1,) + (1,) * (len(shape) - position - 1))

    level = one(*pieces[0])
    for cut in pieces[1:]:
        level = level * one(*cut)
    return level


def bell_draw(own_key, dims, scale, limit, pieces=(), kind=jnp.bfloat16):
    array = jax.random.normal(own_key, dims, jnp.float32) * scale
    if len(pieces) > 0:
        array = block_levels(own_key, dims, pieces, -0.22, 0.18) * array
    return jnp.clip(array, min=-limit, max=limit).astype(kind)


def setup_inputs(seed: int = 0) -> dict:
    keys = jax.random.split(jax.random.key(seed), 5)
    return {
        "rhs": bell_draw(keys[0], (NQ, NRHS, PX, 2, PY), 1.0, 6.0, ((0, 4), (2, 8)), jnp.float32),
        "fronts": bell_draw(keys[1], (NQ, 2, CF, CF), FRONT ** -0.5, 0.046875, ((0, 4), (2, 8))),
        "wave_sq": jnp.clip(0.5 + 1.5 * jax.random.uniform(keys[2], (NQ, PX, PY), jnp.float32) ** block_levels(keys[2], (NQ, PX, PY), ((0, 4), (1, 8)), -0.2, 0.2), 0.5, 2.0),
        "pml_width": place_ends(jax.random.randint(keys[3], (NQ,), 1, PX // 4 + 1), jax.random.fold_in(keys[3], 1), 1, (PX // 4 + 1) - 1).astype(jnp.int32),
    }


def reference(rhs, fronts, wave_sq, pml_width):
    carried = jnp.zeros((NRHS, PX, 2, PY), jnp.float32)
    solved_list = []
    for panel_num in range(NQ):
        combined = (rhs[panel_num] + carried).astype(jnp.bfloat16)
        x_re = combined[:, :, 0].reshape(NRHS, CF)
        x_im = combined[:, :, 1].reshape(NRHS, CF)
        c_re = fronts[panel_num, 0].T
        c_im = fronts[panel_num, 1].T
        out_re = jnp.dot(x_re, c_re, preferred_element_type=jnp.float32) - jnp.dot(x_im, c_im, preferred_element_type=jnp.float32)
        out_im = jnp.dot(x_re, c_im, preferred_element_type=jnp.float32) + jnp.dot(x_im, c_re, preferred_element_type=jnp.float32)
        solved = jnp.stack([out_re.reshape(NRHS, PX, PY), out_im.reshape(NRHS, PX, PY)], axis=2)
        solved_list.append(solved)
        carried = solved
    sweep_field = jnp.stack(solved_list)
    row_pos = jnp.arange(PX, dtype=jnp.float32)[None, :]
    thick = pml_width.astype(jnp.float32)[:, None]
    absorb = 2.0 * (jnp.maximum(0.0, thick - row_pos) + jnp.maximum(0.0, row_pos - (PX - 1 - thick))) / thick
    padded = jnp.pad(sweep_field, ((1, 1), (0, 0), (1, 1), (0, 0), (1, 1)))
    beside = padded[2:, :, 1:-1, :, 1:-1] + padded[:-2, :, 1:-1, :, 1:-1]
    beside = beside + padded[1:-1, :, 2:, :, 1:-1] + padded[1:-1, :, :-2, :, 1:-1]
    beside = beside + padded[1:-1, :, 1:-1, :, 2:] + padded[1:-1, :, 1:-1, :, :-2]
    diagonal_term = (6.0 - wave_sq)[:, None, :, :]
    absorb_b = absorb[:, None, :, None]
    real_part = sweep_field[:, :, :, 0]
    imag_part = sweep_field[:, :, :, 1]
    apply_re = diagonal_term * real_part - absorb_b * imag_part - beside[:, :, :, 0]
    apply_im = diagonal_term * imag_part + absorb_b * real_part - beside[:, :, :, 1]
    residual = rhs - jnp.stack([apply_re, apply_im], axis=3)
    return sweep_field, residual
```

```python
import functools

import jax
import jax.numpy as jnp
from jax import lax
from jax.experimental import pallas as pl
from jax.experimental.pallas import tpu as pltpu
from jax.sharding import PartitionSpec as P


def mul_kernel(first, last, ids_ref, x_ref, c_ref, *refs):
    refs = list(refs)
    acc_in = None if first else refs.pop(0)
    rhs_ref = refs.pop(0) if last else None
    s_ref = refs.pop(0) if last else None
    k = pl.program_id(1)
    count = pl.num_programs(1)

    if last:

        @pl.when(ids_ref[0] == 0)
        def _():
            refs[0][...] = s_ref[...]

    @pl.when(ids_ref[0] == 1)
    def _():
        acc = refs[-1]
        x = x_ref[k]
        re = jnp.dot(c_ref[0, 0], x, preferred_element_type=jnp.float32)
        im = jnp.dot(c_ref[0, 1], x, preferred_element_type=jnp.float32)

        @pl.when(k == 0)
        def _():
            if first:
                acc[0] = re
                acc[1] = im
            else:
                acc[0] = acc_in[0] + re
                acc[1] = acc_in[1] + im

        @pl.when(k > 0)
        def _():
            acc[0] += re
            acc[1] += im

        if last:

            @pl.when(k == count - 1)
            def _():
                half = x.shape[1] // 2
                turn = acc[1]
                s = acc[0] + jnp.concatenate([-turn[:, half:], turn[:, :half]], axis=1)
                refs[0][...] = s
                refs[1][...] = (rhs_ref[...] + s).astype(jnp.bfloat16)


def multiply(ids, x, fronts, acc=None, rhs=None, s=None):
    count, width, lanes = x.shape
    rows = fronts.shape[2]
    tile = min(rows, 512)
    first, last = acc is None, rhs is not None

    def front_block(i, k, ids):
        return (0, 0, i * ids[0], ids[1 + k] * ids[0])

    acc_spec = pl.BlockSpec((2, tile, lanes), lambda i, k, ids: (0, i, 0))
    row_spec = pl.BlockSpec((tile, lanes), lambda i, k, ids: (i, 0))
    operands = [x, fronts]
    in_specs = [
        pl.BlockSpec((count, width, lanes), lambda i, k, ids: (0, 0, 0)),
        pl.BlockSpec((1, 2, tile, width), front_block),
    ]
    if not first:
        operands.append(acc)
        in_specs.append(acc_spec)
    aliases = {}
    scratch = []
    if last:
        operands += [rhs, s]
        in_specs += [row_spec, row_spec]
        aliases = {len(operands): 0}
        out_shape = [
            jax.ShapeDtypeStruct((rows, lanes), jnp.float32),
            jax.ShapeDtypeStruct((rows, lanes), jnp.bfloat16),
        ]
        out_specs = [row_spec, row_spec]
        scratch = [pltpu.VMEM((2, tile, lanes), jnp.float32)]
    else:
        out_shape = jax.ShapeDtypeStruct((2, rows, lanes), jnp.float32)
        out_specs = acc_spec
    flops = 4 * rows * width * count * lanes
    return pl.pallas_call(
        functools.partial(mul_kernel, first, last),
        grid_spec=pltpu.PrefetchScalarGridSpec(
            num_scalar_prefetch=1,
            grid=(rows // tile, count),
            in_specs=in_specs,
            out_specs=out_specs,
            scratch_shapes=scratch,
        ),
        out_shape=out_shape,
        input_output_aliases=aliases,
        compiler_params=pltpu.CompilerParams(vmem_limit_bytes=24 * 1024 * 1024),
        cost_estimate=pl.CostEstimate(
            flops=flops, bytes_accessed=4 * rows * width * count, transcendentals=0
        ),
    )(ids, *operands)


def local(rhs, fronts, wave_sq, pml_width):
    _, rhs_count, row_count, components, columns = rhs.shape
    panels = lax.axis_size("panel")
    front = lax.axis_size("front")
    panel = lax.axis_index("panel")
    place = lax.axis_index("front").astype(jnp.int32)
    rows = row_count * columns
    lanes = components * rhs_count
    masks = [1 << b for b in reversed(range(front.bit_length() - 1))]

    def exchange(values, mask, source, target):
        pairs = [(source * front + (j ^ mask), target * front + j) for j in range(front)]
        return lax.ppermute(values, ("panel", "front"), pairs)

    def shift_panel(values, by):
        pairs = [
            (p * front + j, (p + by) * front + j)
            for p in range(panels)
            for j in range(front)
            if 0 <= p + by < panels
        ]
        return lax.ppermute(values, ("panel", "front"), pairs)

    def chunk_ids(active, offsets):
        return jnp.stack([active] + [place ^ o for o in offsets]).astype(jnp.int32)

    rhs_t = rhs[0].transpose(1, 3, 2, 0).reshape(rows, lanes)
    rhs_next = shift_panel(rhs_t, -1)
    own = rhs_t.astype(jnp.bfloat16)[None]
    s = rhs_t
    for q in range(panels):
        active = (panel == q).astype(jnp.int32)
        there = exchange(own, masks[0], max(q - 1, 0), q)
        here = own if q == 0 else exchange(own, 0, q - 1, q)
        held = jnp.concatenate([here, there])
        offsets = [0, masks[0]]
        fresh, fresh_offsets = held, offsets
        acc = None
        for mask in masks[1:-2]:
            more = exchange(held, mask, q, q)
            acc = multiply(chunk_ids(active, fresh_offsets), fresh, fronts, acc)
            fresh, fresh_offsets = more, [o ^ mask for o in offsets]
            held = jnp.concatenate([held, more])
            offsets = offsets + fresh_offsets
        mask, end = masks[-2:]
        third = exchange(held, mask, q, q)
        beside_held = exchange(held, end, q, q)
        acc = multiply(chunk_ids(active, fresh_offsets), fresh, fronts, acc)
        beside_third = exchange(third, end, q, q)
        third_offsets = [o ^ mask for o in offsets]
        acc = multiply(
            chunk_ids(active, third_offsets + [o ^ end for o in offsets]),
            jnp.concatenate([third, beside_held]),
            fronts,
            acc,
        )
        s, own = multiply(
            chunk_ids(active, [o ^ end for o in third_offsets]),
            beside_third,
            fronts,
            acc,
            rhs_next,
            s,
        )
        own = own[None]

    cells = s.reshape(row_count, columns, lanes)
    narrow = cells.astype(jnp.bfloat16)
    before = shift_panel(narrow, 1).astype(jnp.float32)
    after = shift_panel(narrow, -1).astype(jnp.float32)
    above = lax.ppermute(narrow[-1:], "front", [(j, j + 1) for j in range(front - 1)])
    below = lax.ppermute(narrow[:1], "front", [(j + 1, j) for j in range(front - 1)])
    tall = jnp.concatenate([above.astype(jnp.float32), cells, below.astype(jnp.float32)])
    beside = before + after + tall[2:] + tall[:-2]
    wide = jnp.pad(cells, ((0, 0), (1, 1), (0, 0)))
    beside = beside + wide[:, 2:] + wide[:, :-2]
    plane_rows = place * row_count + jnp.arange(row_count, dtype=jnp.int32)
    row_pos = plane_rows.astype(jnp.float32)
    total_rows = row_count * front
    thick = pml_width.astype(jnp.float32)
    absorb = (
        2.0
        * (jnp.maximum(0.0, thick - row_pos) + jnp.maximum(0.0, row_pos - (total_rows - 1 - thick)))
        / thick
    )
    turned = jnp.concatenate([-cells[:, :, rhs_count:], cells[:, :, :rhs_count]], axis=2)
    applied = (6.0 - wave_sq[0])[:, :, None] * cells + absorb[:, None, None] * turned - beside
    residual = rhs_t.reshape(cells.shape) - applied

    def back(values):
        values = values.reshape(row_count, columns, components, rhs_count)
        return values.transpose(3, 0, 2, 1)[None]

    return (back(cells), back(residual))


def solution(mesh):
    return jax.shard_map(
        local,
        mesh=mesh,
        in_specs=(
            P("panel", None, "front", None, None),
            P("panel", None, "front", None),
            P("panel", "front", None),
            P("panel"),
        ),
        out_specs=(P("panel", None, "front", None, None), P("panel", None, "front", None, None)),
        check_vma=False,
    )
```

```python
import functools

import jax
import jax.numpy as jnp
from jax import lax
from jax.experimental import pallas as pl
from jax.experimental.pallas import tpu as pltpu
from jax.sharding import PartitionSpec as P


VMEM_LIMIT = 40 * 1024 * 1024


def mul_kernel(count, first, last, ids_ref, front_ref, *refs):
    *refs, blocks, sems = refs
    x_refs, refs = refs[:count], list(refs[count:])
    acc_in = None if first else refs.pop(0)
    rhs_ref, s_in = (refs.pop(0), refs.pop(0)) if last else (None, None)

    if last:

        @pl.when(ids_ref[0] == 0)
        def _():
            refs[0][...] = s_in[...]

    @pl.when(ids_ref[0] == 1)
    def _():
        width, lanes = x_refs[0].shape[1:]
        rows = front_ref.shape[2]
        piece = blocks.shape[3]
        copies = []
        for k in range(count):
            for part in range(width // piece):
                begin = pl.multiple_of(ids_ref[1 + k] * width + part * piece, piece)
                slot = len(copies)
                copies.append(
                    pltpu.make_async_copy(
                        front_ref.at[0, :, :, pl.ds(begin, piece)], blocks.at[slot], sems.at[slot]
                    )
                )
                copies[-1].start()
        acc = None if first else acc_in[...].reshape(2 * rows, lanes)
        for slot, copy in enumerate(copies):
            copy.wait()
            k, begin = divmod(slot * piece, width)
            x = x_refs[k][0, begin : begin + piece]
            block = blocks[slot].reshape(2 * rows, piece)
            term = jnp.dot(block, x, preferred_element_type=jnp.float32)
            acc = term if acc is None else acc + term
        if last:
            half = lanes // 2
            re, im = acc[:rows], acc[rows:]
            s = re + jnp.concatenate([-im[:, half:], im[:, :half]], axis=1)
            refs[0][...] = s
            refs[1][0] = (rhs_ref[...] + s).astype(jnp.bfloat16)
        else:
            refs[0][...] = acc.reshape(2, rows, lanes)


def multiply(ids, xs, fronts, acc=None, rhs=None, s=None):
    count = len(xs)
    _, width, lanes = xs[0].shape
    rows = fronts.shape[2]
    first, last = acc is None, rhs is not None
    vmem = pl.BlockSpec(memory_space=pltpu.VMEM)
    piece = width // 2 if last and width % 256 == 0 else width
    pieces = count * width // piece
    operands = [ids, fronts, *xs]
    aliases = {}
    if not first:
        if not last:
            aliases[len(operands)] = 0
        operands.append(acc)
    if last:
        operands += [rhs, s]
        aliases[len(operands) - 1] = 0
        out_shape = [
            jax.ShapeDtypeStruct((rows, lanes), jnp.float32),
            jax.ShapeDtypeStruct((1, rows, lanes), jnp.bfloat16),
        ]
    else:
        out_shape = [jax.ShapeDtypeStruct((2, rows, lanes), jnp.float32)]
    return pl.pallas_call(
        functools.partial(mul_kernel, count, first, last),
        in_specs=[
            pl.BlockSpec(memory_space=pltpu.SMEM),
            pl.BlockSpec(memory_space=pl.ANY),
            *[vmem] * (len(operands) - 2),
        ],
        out_specs=[vmem] * len(out_shape),
        out_shape=out_shape,
        scratch_shapes=[
            pltpu.VMEM((pieces, 2, rows, piece), jnp.bfloat16),
            pltpu.SemaphoreType.DMA((pieces,)),
        ],
        input_output_aliases=aliases,
        compiler_params=pltpu.CompilerParams(vmem_limit_bytes=VMEM_LIMIT),
        cost_estimate=pl.CostEstimate(
            flops=8 * rows * width * count * lanes, bytes_accessed=4 * rows * width * count, transcendentals=0
        ),
    )(*operands)


def local(rhs, fronts, wave_sq, pml_width):
    _, rhs_count, row_count, components, columns = rhs.shape
    panels = lax.axis_size("panel")
    front = lax.axis_size("front")
    panel = lax.axis_index("panel")
    place = lax.axis_index("front").astype(jnp.int32)
    rows = row_count * columns
    lanes = components * rhs_count
    masks = [1 << b for b in reversed(range(front.bit_length() - 1))]

    def exchange(values, mask, source, target):
        pairs = [(source * front + (j ^ mask), target * front + j) for j in range(front)]
        return lax.ppermute(values, ("panel", "front"), pairs)

    def shift_panel(values, by):
        pairs = [
            (p * front + j, (p + by) * front + j)
            for p in range(panels)
            for j in range(front)
            if 0 <= p + by < panels
        ]
        return lax.ppermute(values, ("panel", "front"), pairs)

    def send(values, source, target, mask=0):
        return exchange(values, mask, source, target)

    rhs_t = rhs[0].transpose(1, 3, 2, 0).reshape(rows, lanes)
    near = [masks[-2] | masks[-1], masks[-2], masks[-1], 0]
    own = rhs_t.astype(jnp.bfloat16)[None]
    rhs_next = shift_panel(rhs_t, -1)
    s = rhs_t
    joined = jnp.where(panel == 0, rhs_t, 0.0)
    for q in range(panels):
        active = (panel == q).astype(jnp.int32)
        sender = q ^ 1
        if q % 2 == 0:
            own = send(own, max(q - 1, 0), sender)
        held, offsets = [own], [0]
        arrived, arrived_offsets = [], []

        def deliver(parts, part_offsets):
            for part, offset in zip(parts, part_offsets):
                for mask in near:
                    arrived.append(send(part, sender, q, mask))
                    arrived_offsets.append(offset ^ mask)

        fresh, fresh_offsets = held, offsets
        for mask in masks[:-2]:
            more = [send(part, sender, sender, mask) for part in held]
            deliver(fresh, fresh_offsets)
            fresh, fresh_offsets = more, [o ^ mask for o in offsets]
            held, offsets = held + fresh, offsets + fresh_offsets
        deliver(fresh, fresh_offsets)
        if q > 0:
            joined = joined + arrived[len(near) - 1][0].astype(jnp.float32)

        acc = None
        cuts = list(range(0, len(arrived) - 4, 4)) + [len(arrived) - 4, len(arrived) - 2]
        for begin, end in zip(cuts, cuts[1:] + [len(arrived)]):
            ids = jnp.stack([active] + [place ^ o for o in arrived_offsets[begin:end]])
            xs = arrived[begin:end]
            if end < len(arrived):
                (acc,) = multiply(ids, xs, fronts, acc)
            else:
                s, own = multiply(ids, xs, fronts, acc, rhs_next, s)

    cells = s.reshape(row_count, columns, lanes)
    narrow = cells.astype(jnp.bfloat16)
    after = shift_panel(narrow, -1).astype(jnp.float32)
    above = lax.ppermute(narrow[-1:], "front", [(j, j + 1) for j in range(front - 1)])
    below = lax.ppermute(narrow[:1], "front", [(j + 1, j) for j in range(front - 1)])
    tall = jnp.concatenate([above.astype(jnp.float32), cells, below.astype(jnp.float32)])
    beside = after + tall[2:] + tall[:-2]
    wide = jnp.pad(cells, ((0, 0), (1, 1), (0, 0)))
    beside = beside + wide[:, 2:] + wide[:, :-2]
    plane_rows = place * row_count + jnp.arange(row_count, dtype=jnp.int32)
    row_pos = plane_rows.astype(jnp.float32)
    total_rows = row_count * front
    thick = pml_width.astype(jnp.float32)
    absorb = (
        2.0
        * (jnp.maximum(0.0, thick - row_pos) + jnp.maximum(0.0, row_pos - (total_rows - 1 - thick)))
        / thick
    )
    turned = jnp.concatenate([-cells[:, :, rhs_count:], cells[:, :, :rhs_count]], axis=2)
    applied = (6.0 - wave_sq[0])[:, :, None] * cells + absorb[:, None, None] * turned - beside
    residual = joined.reshape(cells.shape) - applied

    def back(values):
        values = values.reshape(row_count, columns, components, rhs_count)
        return values.transpose(3, 0, 2, 1)[None]

    return (back(cells), back(residual))


def solution(mesh):
    return jax.shard_map(
        local,
        mesh=mesh,
        in_specs=(
            P("panel", None, "front", None, None),
            P("panel", None, "front", None),
            P("panel", "front", None),
            P("panel"),
        ),
        out_specs=(P("panel", None, "front", None, None), P("panel", None, "front", None, None)),
        check_vma=False,
    )
```

```python
import functools

import jax
import jax.numpy as jnp
from jax import lax
from jax.experimental import pallas as pl
from jax.experimental.pallas import tpu as pltpu
from jax.sharding import PartitionSpec as P


VMEM_LIMIT = 40 * 1024 * 1024


def mul_kernel(count, extra, first, last, ids_ref, front_ref, *refs):
    *refs, blocks, sems = refs[extra:]
    x_refs, refs = refs[:count], list(refs[count:])
    acc_in = None if first else refs.pop(0)
    rhs_ref, s_in = (refs.pop(0), refs.pop(0)) if last else (None, None)

    if last:

        @pl.when(ids_ref[0] == 0)
        def _():
            refs[0][...] = s_in[...]

    @pl.when(ids_ref[0] == 1)
    def _():
        width, lanes = x_refs[0].shape[1:]
        rows = front_ref.shape[2]
        piece = blocks.shape[3]
        copies = []
        for slot in range(count * width // piece):
            k, begin = divmod(slot * piece, width)
            begin = pl.multiple_of(ids_ref[1 + k] * width + begin, piece)
            copies.append(
                pltpu.make_async_copy(
                    front_ref.at[0, :, :, pl.ds(begin, piece)], blocks.at[slot], sems.at[slot]
                )
            )
        for copy in copies[:2]:
            copy.start()
        acc = None if first else acc_in[...].reshape(2 * rows, lanes)
        for slot, copy in enumerate(copies):
            copy.wait()
            if slot + 2 < len(copies):
                copies[slot + 2].start()
            k, begin = divmod(slot * piece, width)
            x = x_refs[k][0, begin : begin + piece]
            block = blocks[slot].reshape(2 * rows, piece)
            term = jnp.dot(block, x, preferred_element_type=jnp.float32)
            acc = term if acc is None else acc + term
        if last:
            half = lanes // 2
            re, im = acc[:rows], acc[rows:]
            s = re + jnp.concatenate([-im[:, half:], im[:, :half]], axis=1)
            refs[0][...] = s
            refs[1][0] = (rhs_ref[...] + s).astype(jnp.bfloat16)
        else:
            refs[0][...] = acc.reshape(2, rows, lanes)


def multiply(ids, xs, fronts, after, acc=None, rhs=None, s=None):
    count = len(xs)
    _, width, lanes = xs[0].shape
    rows = fronts.shape[2]
    first, last = acc is None, rhs is not None
    vmem = pl.BlockSpec(memory_space=pltpu.VMEM)
    piece = min(width, 512)
    pieces = count * width // piece
    operands = [ids, fronts, *after, *xs]
    aliases = {}
    if not first:
        if not last:
            aliases[len(operands)] = 0
        operands.append(acc)
    if last:
        operands += [rhs, s]
        aliases[len(operands) - 1] = 0
        out_shape = [
            jax.ShapeDtypeStruct((rows, lanes), jnp.float32),
            jax.ShapeDtypeStruct((1, rows, lanes), jnp.bfloat16),
        ]
    else:
        out_shape = [jax.ShapeDtypeStruct((2, rows, lanes), jnp.float32)]
    return pl.pallas_call(
        functools.partial(mul_kernel, count, len(after), first, last),
        in_specs=[
            pl.BlockSpec(memory_space=pltpu.SMEM),
            *[pl.BlockSpec(memory_space=pl.ANY)] * (1 + len(after)),
            *[vmem] * (len(operands) - 2 - len(after)),
        ],
        out_specs=[vmem] * len(out_shape),
        out_shape=out_shape,
        scratch_shapes=[
            pltpu.VMEM((pieces, 2, rows, piece), jnp.bfloat16),
            pltpu.SemaphoreType.DMA((pieces,)),
        ],
        input_output_aliases=aliases,
        compiler_params=pltpu.CompilerParams(vmem_limit_bytes=VMEM_LIMIT),
        cost_estimate=pl.CostEstimate(
            flops=8 * rows * width * count * lanes, bytes_accessed=4 * rows * width * count, transcendentals=0
        ),
    )(*operands)


def local(rhs, fronts, wave_sq, pml_width):
    _, rhs_count, row_count, components, columns = rhs.shape
    panels = lax.axis_size("panel")
    front = lax.axis_size("front")
    panel = lax.axis_index("panel")
    place = lax.axis_index("front").astype(jnp.int32)
    rows = row_count * columns
    lanes = components * rhs_count
    masks = [1 << b for b in reversed(range(front.bit_length() - 1))]

    def exchange(values, mask, source, target):
        pairs = [(source * front + (j ^ mask), target * front + j) for j in range(front)]
        return lax.ppermute(values, ("panel", "front"), pairs)

    def shift_panel(values, by):
        pairs = [
            (p * front + j, (p + by) * front + j)
            for p in range(panels)
            for j in range(front)
            if 0 <= p + by < panels
        ]
        return lax.ppermute(values, ("panel", "front"), pairs)

    def send(values, source, target, mask=0):
        return exchange(values, mask, source, target)

    rhs_t = rhs[0].transpose(1, 3, 2, 0).reshape(rows, lanes)
    near = [0, masks[-2], masks[-1], masks[-2] | masks[-1]]
    own = rhs_t.astype(jnp.bfloat16)[None]
    rhs_next = shift_panel(rhs_t, -1)
    s = rhs_t
    joined = jnp.where(panel == 0, rhs_t, 0.0)
    for q in range(panels):
        active = (panel == q).astype(jnp.int32)
        sender = q ^ 1
        if q % 2 == 0:
            own = send(own, max(q - 1, 0), sender)
        held, offsets = [own], [0]
        arrived, arrived_offsets = [], []

        def deliver(parts, part_offsets):
            for part, offset in zip(parts, part_offsets):
                for mask in near:
                    arrived.append(send(part, sender, q, mask))
                    arrived_offsets.append(offset ^ mask)

        fresh, fresh_offsets = held, offsets
        for mask in masks[:-2]:
            more = [send(part, sender, sender, mask) for part in held]
            deliver(fresh, fresh_offsets)
            fresh, fresh_offsets = more, [o ^ mask for o in offsets]
            held, offsets = held + fresh, offsets + fresh_offsets
        deliver(fresh, fresh_offsets)
        if q > 0:
            joined = joined + arrived[0][0].astype(jnp.float32)

        acc = None
        cuts = list(range(0, len(arrived), max(2, len(arrived) // 4)))
        for begin, end in zip(cuts, cuts[1:] + [len(arrived)]):
            ids = jnp.stack([active] + [place ^ o for o in arrived_offsets[begin:end]])
            xs = arrived[begin:end]
            after = fresh if begin == 0 else []
            if end < len(arrived):
                (acc,) = multiply(ids, xs, fronts, after, acc)
            else:
                s, own = multiply(ids, xs, fronts, after, acc, rhs_next, s)

    cells = s.reshape(row_count, columns, lanes)
    narrow = cells.astype(jnp.bfloat16)
    after = shift_panel(narrow, -1).astype(jnp.float32)
    above = lax.ppermute(narrow[-1:], "front", [(j, j + 1) for j in range(front - 1)])
    below = lax.ppermute(narrow[:1], "front", [(j + 1, j) for j in range(front - 1)])
    tall = jnp.concatenate([above.astype(jnp.float32), cells, below.astype(jnp.float32)])
    beside = after + tall[2:] + tall[:-2]
    wide = jnp.pad(cells, ((0, 0), (1, 1), (0, 0)))
    beside = beside + wide[:, 2:] + wide[:, :-2]
    plane_rows = place * row_count + jnp.arange(row_count, dtype=jnp.int32)
    row_pos = plane_rows.astype(jnp.float32)
    total_rows = row_count * front
    thick = pml_width.astype(jnp.float32)
    absorb = (
        2.0
        * (jnp.maximum(0.0, thick - row_pos) + jnp.maximum(0.0, row_pos - (total_rows - 1 - thick)))
        / thick
    )
    turned = jnp.concatenate([-cells[:, :, rhs_count:], cells[:, :, :rhs_count]], axis=2)
    applied = (6.0 - wave_sq[0])[:, :, None] * cells + absorb[:, None, None] * turned - beside
    residual = joined.reshape(cells.shape) - applied

    def back(values):
        values = values.reshape(row_count, columns, components, rhs_count)
        return values.transpose(3, 0, 2, 1)[None]

    return (back(cells), back(residual))


def solution(mesh):
    return jax.shard_map(
        local,
        mesh=mesh,
        in_specs=(
            P("panel", None, "front", None, None),
            P("panel", None, "front", None),
            P("panel", "front", None),
            P("panel"),
        ),
        out_specs=(P("panel", None, "front", None, None), P("panel", None, "front", None, None)),
        check_vma=False,
    )
```

```python
import functools

import jax
import jax.numpy as jnp
from jax import lax
from jax.experimental import pallas as pl
from jax.experimental.pallas import tpu as pltpu
from jax.sharding import PartitionSpec as P


VMEM_LIMIT = 40 * 1024 * 1024
ROW_TILE = 512


def mul_kernel(count, extra, first, last, ids_ref, front_ref, *refs):
    *refs, blocks, sems = refs[extra:]
    x_refs, refs = refs[:count], list(refs[count:])
    acc_in = None if first else refs.pop(0)
    rhs_ref, s_in = (refs.pop(0), refs.pop(0)) if last else (None, None)

    if last:

        @pl.when(ids_ref[0] == 0)
        def _():
            refs[0][...] = s_in[...]

    @pl.when(ids_ref[0] == 1)
    def _():
        width, lanes = x_refs[0].shape[1:]
        slots, tile, _ = blocks.shape
        rows = front_ref.shape[2]
        order = [(part, begin) for begin in range(0, rows, tile) for part in range(2)]

        def copies(step):
            part, begin = order[step]
            return [
                pltpu.make_async_copy(
                    front_ref.at[
                        0,
                        part,
                        pl.ds(begin, tile),
                        pl.ds(pl.multiple_of(ids_ref[1 + k] * width, width), width),
                    ],
                    blocks.at[step % slots, :, pl.ds(k * width, width)],
                    sems.at[step % slots, k],
                )
                for k in range(count)
            ]

        def fetch(step):
            if step < len(order):
                for copy in copies(step):
                    copy.start()

        for step in range(slots):
            fetch(step)
        x = jnp.concatenate([x_ref[0] for x_ref in x_refs])
        for step, (part, begin) in enumerate(order):
            for copy in copies(step):
                copy.wait()
            term = jnp.dot(blocks[step % slots], x, preferred_element_type=jnp.float32)
            fetch(step + slots)
            if not first:
                term = term + acc_in[part, begin : begin + tile]
            if not last:
                refs[0][part, begin : begin + tile] = term
            elif part == 0:
                re = term
            else:
                half = lanes // 2
                s = re + jnp.concatenate([-term[:, half:], term[:, :half]], axis=1)
                refs[0][begin : begin + tile] = s
                refs[1][0, begin : begin + tile] = (rhs_ref[begin : begin + tile] + s).astype(
                    jnp.bfloat16
                )


def multiply(ids, xs, fronts, after, acc=None, rhs=None, s=None):
    count = len(xs)
    _, width, lanes = xs[0].shape
    rows = fronts.shape[2]
    first, last = acc is None, rhs is not None
    vmem = pl.BlockSpec(memory_space=pltpu.VMEM)
    tile = min(rows, ROW_TILE)
    slots = min(3, 2 * rows // tile)
    operands = [ids, fronts, *after, *xs]
    aliases = {}
    if not first:
        if not last:
            aliases[len(operands)] = 0
        operands.append(acc)
    if last:
        operands += [rhs, s]
        aliases[len(operands) - 1] = 0
        out_shape = [
            jax.ShapeDtypeStruct((rows, lanes), jnp.float32),
            jax.ShapeDtypeStruct((1, rows, lanes), jnp.bfloat16),
        ]
    else:
        out_shape = [jax.ShapeDtypeStruct((2, rows, lanes), jnp.float32)]
    return pl.pallas_call(
        functools.partial(mul_kernel, count, len(after), first, last),
        in_specs=[
            pl.BlockSpec(memory_space=pltpu.SMEM),
            *[pl.BlockSpec(memory_space=pl.ANY)] * (1 + len(after)),
            *[vmem] * (len(operands) - 2 - len(after)),
        ],
        out_specs=[vmem] * len(out_shape),
        out_shape=out_shape,
        scratch_shapes=[
            pltpu.VMEM((slots, tile, count * width), jnp.bfloat16),
            pltpu.SemaphoreType.DMA((slots, count)),
        ],
        input_output_aliases=aliases,
        compiler_params=pltpu.CompilerParams(vmem_limit_bytes=VMEM_LIMIT),
        cost_estimate=pl.CostEstimate(
            flops=8 * rows * width * count * lanes, bytes_accessed=4 * rows * width * count, transcendentals=0
        ),
    )(*operands)


def local(rhs, fronts, wave_sq, pml_width):
    _, rhs_count, row_count, components, columns = rhs.shape
    panels = lax.axis_size("panel")
    front = lax.axis_size("front")
    panel = lax.axis_index("panel")
    place = lax.axis_index("front").astype(jnp.int32)
    rows = row_count * columns
    lanes = components * rhs_count
    masks = [1 << b for b in reversed(range(front.bit_length() - 1))]

    def exchange(values, mask, source, target):
        pairs = [(source * front + (j ^ mask), target * front + j) for j in range(front)]
        return lax.ppermute(values, ("panel", "front"), pairs)

    def shift_panel(values, by):
        pairs = [
            (p * front + j, (p + by) * front + j)
            for p in range(panels)
            for j in range(front)
            if 0 <= p + by < panels
        ]
        return lax.ppermute(values, ("panel", "front"), pairs)

    def send(values, source, target, mask=0):
        return exchange(values, mask, source, target)

    rhs_t = rhs[0].transpose(1, 3, 2, 0).reshape(rows, lanes)
    near = [0, masks[-2], masks[-1], masks[-2] | masks[-1]]
    own = rhs_t.astype(jnp.bfloat16)[None]
    rhs_next = shift_panel(rhs_t, -1)
    s = rhs_t
    joined = jnp.where(panel == 0, rhs_t, 0.0)
    for q in range(panels):
        active = (panel == q).astype(jnp.int32)
        sender = q ^ 1
        if q % 2 == 0:
            own = send(own, max(q - 1, 0), sender)
        held, offsets = [own], [0]
        arrived, arrived_offsets = [], []

        def deliver(parts, part_offsets):
            for part, offset in zip(parts, part_offsets):
                for mask in near:
                    arrived.append(send(part, sender, q, mask))
                    arrived_offsets.append(offset ^ mask)

        fresh, fresh_offsets = held, offsets
        for mask in masks[:-2]:
            deliver(fresh, fresh_offsets)
            fresh = [send(part, sender, sender, mask) for part in held]
            fresh_offsets = [o ^ mask for o in offsets]
            held, offsets = held + fresh, offsets + fresh_offsets
        deliver(fresh, fresh_offsets)
        if q > 0:
            joined = joined + arrived[0][0].astype(jnp.float32)

        acc = None
        cuts = list(range(0, len(arrived), max(2, len(arrived) // 4)))
        for begin, end in zip(cuts, cuts[1:] + [len(arrived)]):
            ids = jnp.stack([active] + [place ^ o for o in arrived_offsets[begin:end]])
            xs = arrived[begin:end]
            after = fresh if begin == 0 else []
            if end < len(arrived):
                (acc,) = multiply(ids, xs, fronts, after, acc)
            else:
                s, own = multiply(ids, xs, fronts, after, acc, rhs_next, s)

    cells = s.reshape(row_count, columns, lanes)
    narrow = cells.astype(jnp.bfloat16)
    after = shift_panel(narrow, -1).astype(jnp.float32)
    above = lax.ppermute(narrow[-1:], "front", [(j, j + 1) for j in range(front - 1)])
    below = lax.ppermute(narrow[:1], "front", [(j + 1, j) for j in range(front - 1)])
    tall = jnp.concatenate([above.astype(jnp.float32), cells, below.astype(jnp.float32)])
    beside = after + tall[2:] + tall[:-2]
    wide = jnp.pad(cells, ((0, 0), (1, 1), (0, 0)))
    beside = beside + wide[:, 2:] + wide[:, :-2]
    plane_rows = place * row_count + jnp.arange(row_count, dtype=jnp.int32)
    row_pos = plane_rows.astype(jnp.float32)
    total_rows = row_count * front
    thick = pml_width.astype(jnp.float32)
    absorb = (
        2.0
        * (jnp.maximum(0.0, thick - row_pos) + jnp.maximum(0.0, row_pos - (total_rows - 1 - thick)))
        / thick
    )
    turned = jnp.concatenate([-cells[:, :, rhs_count:], cells[:, :, :rhs_count]], axis=2)
    applied = (6.0 - wave_sq[0])[:, :, None] * cells + absorb[:, None, None] * turned - beside
    residual = joined.reshape(cells.shape) - applied

    def back(values):
        values = values.reshape(row_count, columns, components, rhs_count)
        return values.transpose(3, 0, 2, 1)[None]

    return (back(cells), back(residual))


def solution(mesh):
    return jax.shard_map(
        local,
        mesh=mesh,
        in_specs=(
            P("panel", None, "front", None, None),
            P("panel", None, "front", None),
            P("panel", "front", None),
            P("panel"),
        ),
        out_specs=(P("panel", None, "front", None, None), P("panel", None, "front", None, None)),
        check_vma=False,
    )
```

```python
import functools

import jax
import jax.numpy as jnp
from jax import lax
from jax.experimental import pallas as pl
from jax.experimental.pallas import tpu as pltpu
from jax.sharding import PartitionSpec as P


VMEM_LIMIT = 40 * 1024 * 1024
ROW_TILE = 512


def mul_kernel(count, extra, first, last, ids_ref, front_ref, *refs):
    *refs, blocks, x_all, sems = refs[extra:]
    x_refs, refs = refs[:count], list(refs[count:])
    acc_in = None if first else refs.pop(0)
    rhs_ref, s_in = (refs.pop(0), refs.pop(0)) if last else (None, None)

    if last:

        @pl.when(ids_ref[0] == 0)
        def _():
            refs[0][...] = s_in[...]

    @pl.when(ids_ref[0] == 1)
    def _():
        width, lanes = x_refs[0].shape[1:]
        slots, tile, _ = blocks.shape
        rows = front_ref.shape[2]
        order = [(part, begin) for begin in range(0, rows, tile) for part in range(2)]

        def copy(step):
            part, begin = order[step]
            base = pl.multiple_of(ids_ref[1] * width, width)
            return pltpu.make_async_copy(
                front_ref.at[0, part, pl.ds(begin, tile), pl.ds(base, count * width)],
                blocks.at[step % slots],
                sems.at[step % slots],
            )

        def fetch(step):
            if step < len(order):
                copy(step).start()

        for step in range(slots):
            fetch(step)
        for k in range(count):
            place = pl.multiple_of(ids_ref[2 + k] * width, width)
            x_all[pl.ds(place, width)] = x_refs[k][0]
        for step, (part, begin) in enumerate(order):
            copy(step).wait()
            term = jnp.dot(blocks[step % slots], x_all[...], preferred_element_type=jnp.float32)
            fetch(step + slots)
            if not first:
                term = term + acc_in[part, begin : begin + tile]
            if not last:
                refs[0][part, begin : begin + tile] = term
            elif part == 0:
                re = term
            else:
                half = lanes // 2
                s = re + jnp.concatenate([-term[:, half:], term[:, :half]], axis=1)
                refs[0][begin : begin + tile] = s
                refs[1][0, begin : begin + tile] = (rhs_ref[begin : begin + tile] + s).astype(
                    jnp.bfloat16
                )


def multiply(ids, xs, fronts, after, acc=None, rhs=None, s=None):
    count = len(xs)
    _, width, lanes = xs[0].shape
    rows = fronts.shape[2]
    first, last = acc is None, rhs is not None
    vmem = pl.BlockSpec(memory_space=pltpu.VMEM)
    tile = min(rows, ROW_TILE)
    slots = 2
    operands = [ids, fronts, *after, *xs]
    aliases = {}
    if not first:
        if not last:
            aliases[len(operands)] = 0
        operands.append(acc)
    if last:
        operands += [rhs, s]
        aliases[len(operands) - 1] = 0
        out_shape = [
            jax.ShapeDtypeStruct((rows, lanes), jnp.float32),
            jax.ShapeDtypeStruct((1, rows, lanes), jnp.bfloat16),
        ]
    else:
        out_shape = [jax.ShapeDtypeStruct((2, rows, lanes), jnp.float32)]
    return pl.pallas_call(
        functools.partial(mul_kernel, count, len(after), first, last),
        in_specs=[
            pl.BlockSpec(memory_space=pltpu.SMEM),
            *[pl.BlockSpec(memory_space=pl.ANY)] * (1 + len(after)),
            *[vmem] * (len(operands) - 2 - len(after)),
        ],
        out_specs=[vmem] * len(out_shape),
        out_shape=out_shape,
        scratch_shapes=[
            pltpu.VMEM((slots, tile, count * width), jnp.bfloat16),
            pltpu.VMEM((count * width, lanes), jnp.bfloat16),
            pltpu.SemaphoreType.DMA((slots,)),
        ],
        input_output_aliases=aliases,
        compiler_params=pltpu.CompilerParams(vmem_limit_bytes=VMEM_LIMIT),
        cost_estimate=pl.CostEstimate(
            flops=8 * rows * width * count * lanes, bytes_accessed=4 * rows * width * count, transcendentals=0
        ),
    )(*operands)


def local(rhs, fronts, wave_sq, pml_width):
    _, rhs_count, row_count, components, columns = rhs.shape
    panels = lax.axis_size("panel")
    front = lax.axis_size("front")
    panel = lax.axis_index("panel")
    place = lax.axis_index("front").astype(jnp.int32)
    rows = row_count * columns
    lanes = components * rhs_count
    masks = [1 << b for b in reversed(range(front.bit_length() - 1))]

    def exchange(values, mask, source, target):
        pairs = [(source * front + (j ^ mask), target * front + j) for j in range(front)]
        return lax.ppermute(values, ("panel", "front"), pairs)

    def shift_panel(values, by):
        pairs = [
            (p * front + j, (p + by) * front + j)
            for p in range(panels)
            for j in range(front)
            if 0 <= p + by < panels
        ]
        return lax.ppermute(values, ("panel", "front"), pairs)

    def send(values, source, target, mask=0):
        return exchange(values, mask, source, target)

    rhs_t = rhs[0].transpose(1, 3, 2, 0).reshape(rows, lanes)
    near = [0, masks[-2], masks[-1], masks[-2] | masks[-1]]
    own = rhs_t.astype(jnp.bfloat16)[None]
    rhs_next = shift_panel(rhs_t, -1)
    s = rhs_t
    joined = jnp.where(panel == 0, rhs_t, 0.0)
    for q in range(panels):
        active = (panel == q).astype(jnp.int32)
        sender = q ^ 1
        if q % 2 == 0:
            own = send(own, max(q - 1, 0), sender)
        held, offsets = [own], [0]
        arrived, arrived_offsets = [], []

        def deliver(parts, part_offsets):
            for part, offset in zip(parts, part_offsets):
                for mask in near:
                    arrived.append(send(part, sender, q, mask))
                    arrived_offsets.append(offset ^ mask)

        fresh, fresh_offsets = held, offsets
        for mask in masks[:-2]:
            deliver(fresh, fresh_offsets)
            fresh = [send(part, sender, sender, mask) for part in held]
            fresh_offsets = [o ^ mask for o in offsets]
            held, offsets = held + fresh, offsets + fresh_offsets
        deliver(fresh, fresh_offsets)
        if q > 0:
            joined = joined + arrived[0][0].astype(jnp.float32)

        acc = None
        group = len(near)
        for begin in range(0, len(arrived), group):
            chunks = [place ^ o for o in arrived_offsets[begin : begin + group]]
            ids = jnp.stack([active, chunks[0] // group * group] + [c % group for c in chunks])
            xs = arrived[begin : begin + group]
            after = fresh if begin == 0 else []
            if begin + group < len(arrived):
                (acc,) = multiply(ids, xs, fronts, after, acc)
            else:
                s, own = multiply(ids, xs, fronts, after, acc, rhs_next, s)

    cells = s.reshape(row_count, columns, lanes)
    narrow = cells.astype(jnp.bfloat16)
    after = shift_panel(narrow, -1).astype(jnp.float32)
    above = lax.ppermute(narrow[-1:], "front", [(j, j + 1) for j in range(front - 1)])
    below = lax.ppermute(narrow[:1], "front", [(j + 1, j) for j in range(front - 1)])
    tall = jnp.concatenate([above.astype(jnp.float32), cells, below.astype(jnp.float32)])
    beside = after + tall[2:] + tall[:-2]
    wide = jnp.pad(cells, ((0, 0), (1, 1), (0, 0)))
    beside = beside + wide[:, 2:] + wide[:, :-2]
    plane_rows = place * row_count + jnp.arange(row_count, dtype=jnp.int32)
    row_pos = plane_rows.astype(jnp.float32)
    total_rows = row_count * front
    thick = pml_width.astype(jnp.float32)
    absorb = (
        2.0
        * (jnp.maximum(0.0, thick - row_pos) + jnp.maximum(0.0, row_pos - (total_rows - 1 - thick)))
        / thick
    )
    turned = jnp.concatenate([-cells[:, :, rhs_count:], cells[:, :, :rhs_count]], axis=2)
    applied = (6.0 - wave_sq[0])[:, :, None] * cells + absorb[:, None, None] * turned - beside
    residual = joined.reshape(cells.shape) - applied

    def back(values):
        values = values.reshape(row_count, columns, components, rhs_count)
        return values.transpose(3, 0, 2, 1)[None]

    return (back(cells), back(residual))


def solution(mesh):
    return jax.shard_map(
        local,
        mesh=mesh,
        in_specs=(
            P("panel", None, "front", None, None),
            P("panel", None, "front", None),
            P("panel", "front", None),
            P("panel"),
        ),
        out_specs=(P("panel", None, "front", None, None), P("panel", None, "front", None, None)),
        check_vma=False,
    )
```

```python
import functools

import jax
import jax.numpy as jnp
from jax import lax
from jax.experimental import pallas as pl
from jax.experimental.pallas import tpu as pltpu
from jax.sharding import PartitionSpec as P


VMEM_LIMIT = 5 * 1024 * 1024


def load_kernel(extra, ids_ref, front_ref, *refs):
    *block_refs, sems = refs[extra:]

    @pl.when(ids_ref[0] == 1)
    def _():
        _, rows, width = block_refs[0].shape
        copies = []
        for slot in range(2 * len(block_refs)):
            pair, part = divmod(slot, 2)
            base = pl.multiple_of(ids_ref[1 + pair], width)
            columns = front_ref.at[0, part, :, pl.ds(base, width)]
            copies.append(
                pltpu.make_async_copy(columns, block_refs[pair].at[part], sems.at[slot])
            )
        for copy in copies:
            copy.start()
        for copy in copies:
            copy.wait()


def mul_kernel(pairs, first, last, ids_ref, *refs):
    *refs, x_all = refs
    block_refs, x_refs, refs = refs[:pairs], refs[pairs : 3 * pairs], list(refs[3 * pairs :])
    acc_in = None if first else refs.pop(0)
    rhs_ref, s_in = (refs.pop(0), refs.pop(0)) if last else (None, None)

    if last:

        @pl.when(ids_ref[0] == 0)
        def _():
            refs[0][...] = s_in[...]

    @pl.when(ids_ref[0] == 1)
    def _():
        width, lanes = x_refs[0].shape[1:]
        rows = block_refs[0].shape[1]
        depth = 2 * width
        for k, x_ref in enumerate(x_refs):
            x_all[k // 2, pl.ds(pl.multiple_of(ids_ref[1 + k] * width, width), width)] = x_ref[0]
        term = None
        for pair, block_ref in enumerate(block_refs):
            block = block_ref[...].reshape(2 * rows, depth)
            product = jnp.dot(block, x_all[pair], preferred_element_type=jnp.float32)
            term = product if term is None else term + product
        if not first:
            term = term + acc_in[...].reshape(2 * rows, lanes)
        if not last:
            refs[0][...] = term.reshape(2, rows, lanes)
        else:
            half = lanes // 2
            re, im = term[:rows], term[rows:]
            s = re + jnp.concatenate([-im[:, half:], im[:, :half]], axis=1)
            refs[0][...] = s
            refs[1][0] = (rhs_ref[...] + s).astype(jnp.bfloat16)


def load(active, bases, fronts, width, after):
    ids = jnp.stack([active] + bases)
    rows = fronts.shape[2]
    count = len(bases)
    return pl.pallas_call(
        functools.partial(load_kernel, len(after)),
        in_specs=[
            pl.BlockSpec(memory_space=pltpu.SMEM),
            *[pl.BlockSpec(memory_space=pl.ANY)] * (1 + len(after)),
        ],
        out_specs=[pl.BlockSpec(memory_space=pltpu.VMEM)] * count,
        out_shape=[pltpu.VMEM((2, rows, width), fronts.dtype)] * count,
        scratch_shapes=[pltpu.SemaphoreType.DMA((2 * count,))],
        compiler_params=pltpu.CompilerParams(vmem_limit_bytes=VMEM_LIMIT),
        cost_estimate=pl.CostEstimate(
            flops=0, bytes_accessed=4 * rows * width * count, transcendentals=0
        ),
    )(ids, fronts, *after)


def multiply(ids, xs, blocks, acc=None, rhs=None, s=None):
    pairs = len(blocks)
    _, width, lanes = xs[0].shape
    rows = blocks[0].shape[1]
    first, last = acc is None, rhs is not None
    vmem = pl.BlockSpec(memory_space=pltpu.VMEM)
    smem = pl.BlockSpec(memory_space=pltpu.SMEM)
    blocks = [pltpu.with_memory_space_constraint(block, pltpu.VMEM) for block in blocks]
    operands = [ids, *blocks, *xs]
    aliases = {}
    if not first:
        if not last:
            aliases[len(operands)] = 0
        operands.append(acc)
    if last:
        operands += [rhs, s]
        aliases[len(operands) - 1] = 0
        out_shape = [
            jax.ShapeDtypeStruct((rows, lanes), jnp.float32),
            jax.ShapeDtypeStruct((1, rows, lanes), jnp.bfloat16),
        ]
    else:
        out_shape = [jax.ShapeDtypeStruct((2, rows, lanes), jnp.float32)]
    return pl.pallas_call(
        functools.partial(mul_kernel, pairs, first, last),
        in_specs=[smem, *[vmem] * (len(operands) - 1)],
        out_specs=[vmem] * len(out_shape),
        out_shape=out_shape,
        scratch_shapes=[pltpu.VMEM((pairs, 2 * width, lanes), jnp.bfloat16)],
        input_output_aliases=aliases,
        compiler_params=pltpu.CompilerParams(vmem_limit_bytes=VMEM_LIMIT),
        cost_estimate=pl.CostEstimate(
            flops=16 * rows * width * pairs * lanes, bytes_accessed=0, transcendentals=0
        ),
    )(*operands)


def local(rhs, fronts, wave_sq, pml_width):
    _, rhs_count, row_count, components, columns = rhs.shape
    panels = lax.axis_size("panel")
    front = lax.axis_size("front")
    panel = lax.axis_index("panel")
    place = lax.axis_index("front").astype(jnp.int32)
    rows = row_count * columns
    lanes = components * rhs_count
    masks = [1 << b for b in reversed(range(front.bit_length() - 1))]

    def exchange(values, mask, source, target):
        pairs = [(source * front + (j ^ mask), target * front + j) for j in range(front)]
        return lax.ppermute(values, ("panel", "front"), pairs)

    def shift_panel(values, by):
        pairs = [
            (p * front + j, (p + by) * front + j)
            for p in range(panels)
            for j in range(front)
            if 0 <= p + by < panels
        ]
        return lax.ppermute(values, ("panel", "front"), pairs)

    def send(values, source, target, mask=0):
        return exchange(values, mask, source, target)

    rhs_t = rhs[0].transpose(1, 3, 2, 0).reshape(rows, lanes)
    near = [0, masks[-1], masks[-2], masks[-2] | masks[-1]]
    own = rhs_t.astype(jnp.bfloat16)[None]
    rhs_next = shift_panel(rhs_t, -1)
    s = rhs_t
    joined = jnp.where(panel == 0, rhs_t, 0.0)
    for q in range(panels):
        active = (panel == q).astype(jnp.int32)
        sender = q ^ 1
        if q % 2 == 0:
            own = send(own, max(q - 1, 0), sender)
        held, offsets = [own], [0]
        arrived, arrived_offsets = [], []

        def deliver(parts, part_offsets):
            for part, offset in zip(parts, part_offsets):
                for mask in near:
                    arrived.append(send(part, sender, q, mask))
                    arrived_offsets.append(offset ^ mask)

        fresh, fresh_offsets = held, offsets
        for mask in masks[:-2]:
            deliver(fresh, fresh_offsets)
            fresh = [send(part, sender, sender, mask) for part in held]
            fresh_offsets = [o ^ mask for o in offsets]
            held, offsets = held + fresh, offsets + fresh_offsets
        deliver(fresh, fresh_offsets)
        if q > 0:
            joined = joined + arrived[0][0].astype(jnp.float32)

        acc = None
        chunks = [place ^ o for o in arrived_offsets]
        bases = [chunk // 2 * 2 * rows for chunk in chunks[::2]]
        blocks = load(active, bases, fronts, 2 * rows, fresh)
        cuts = list(range(len(bases)))
        for begin, end in zip(cuts, cuts[1:] + [len(bases)]):
            ids = jnp.stack([active] + [chunk % 2 for chunk in chunks[2 * begin : 2 * end]])
            xs = arrived[2 * begin : 2 * end]
            if end < len(bases):
                (acc,) = multiply(ids, xs, blocks[begin:end], acc)
            else:
                s, own = multiply(ids, xs, blocks[begin:end], acc, rhs_next, s)

    cells = s.reshape(row_count, columns, lanes)
    narrow = cells.astype(jnp.bfloat16)
    after = shift_panel(narrow, -1).astype(jnp.float32)
    above = lax.ppermute(narrow[-1:], "front", [(j, j + 1) for j in range(front - 1)])
    below = lax.ppermute(narrow[:1], "front", [(j + 1, j) for j in range(front - 1)])
    tall = jnp.concatenate([above.astype(jnp.float32), cells, below.astype(jnp.float32)])
    beside = after + tall[2:] + tall[:-2]
    wide = jnp.pad(cells, ((0, 0), (1, 1), (0, 0)))
    beside = beside + wide[:, 2:] + wide[:, :-2]
    plane_rows = place * row_count + jnp.arange(row_count, dtype=jnp.int32)
    row_pos = plane_rows.astype(jnp.float32)
    total_rows = row_count * front
    thick = pml_width.astype(jnp.float32)
    absorb = (
        2.0
        * (jnp.maximum(0.0, thick - row_pos) + jnp.maximum(0.0, row_pos - (total_rows - 1 - thick)))
        / thick
    )
    turned = jnp.concatenate([-cells[:, :, rhs_count:], cells[:, :, :rhs_count]], axis=2)
    applied = (6.0 - wave_sq[0])[:, :, None] * cells + absorb[:, None, None] * turned - beside
    residual = joined.reshape(cells.shape) - applied

    def back(values):
        values = values.reshape(row_count, columns, components, rhs_count)
        return values.transpose(3, 0, 2, 1)[None]

    return (back(cells), back(residual))


def solution(mesh):
    return jax.shard_map(
        local,
        mesh=mesh,
        in_specs=(
            P("panel", None, "front", None, None),
            P("panel", None, "front", None),
            P("panel", "front", None),
            P("panel"),
        ),
        out_specs=(P("panel", None, "front", None, None), P("panel", None, "front", None, None)),
        check_vma=False,
    )
```

```python
import functools

import jax
import jax.numpy as jnp
from jax import lax
from jax.experimental import pallas as pl
from jax.experimental.pallas import tpu as pltpu
from jax.sharding import PartitionSpec as P


VMEM_LIMIT = 5 * 1024 * 1024


def pair_copies(base, front_ref, block_ref, sems):
    _, rows, width = block_ref.shape
    half = rows // 2
    return [
        pltpu.make_async_copy(
            front_ref.at[0, part, pl.ds(begin, half), pl.ds(pl.multiple_of(base, width), width)],
            block_ref.at[part, pl.ds(begin, half)],
            sems.at[2 * part + begin // half],
        )
        for part in range(2)
        for begin in (0, half)
    ]


def load_kernel(extra, ids_ref, front_ref, *refs):
    block_ref, sems = refs[extra:]

    @pl.when(ids_ref[0] == 1)
    def _():
        copies = pair_copies(ids_ref[1], front_ref, block_ref, sems)
        for copy in copies:
            copy.start()
        for copy in copies:
            copy.wait()


def mul_kernel(first, last, ids_ref, front_ref, block_ref, *refs):
    *refs, x_all, sems = refs
    x_refs, refs = refs[:2], list(refs[2:])
    acc_in = None if first else refs.pop(0)
    if last:
        rhs_ref, *kept = refs[:5]
        own_ref, *outs = refs[5:]

        @pl.when(ids_ref[0] == 0)
        def _():
            for out, keep in zip(outs, kept):
                out[...] = keep[...]

    @pl.when(ids_ref[0] == 1)
    def _():
        width, lanes = x_refs[0].shape[1:]
        rows = block_ref.shape[1]
        copies = []
        if not last:
            copies = pair_copies(ids_ref[3], front_ref, refs[1], sems)
        for copy in copies:
            copy.start()
        for k, x_ref in enumerate(x_refs):
            x_all[pl.ds(pl.multiple_of(ids_ref[1 + k] * width, width), width)] = x_ref[0]
        block = block_ref[...].reshape(2 * rows, 2 * width)
        term = jnp.dot(block, x_all[...], preferred_element_type=jnp.float32)
        if not first:
            term = term + acc_in[...].reshape(2 * rows, lanes)
        if not last:
            refs[0][...] = term.reshape(2, rows, lanes)
        else:
            half = lanes // 2
            edge = outs[2].shape[0]
            re, im = term[:rows], term[rows:]
            s = re + jnp.concatenate([-im[:, half:], im[:, :half]], axis=1)
            narrow = s.astype(jnp.bfloat16)
            own_ref[0] = (rhs_ref[...] + s).astype(jnp.bfloat16)
            outs[0][...] = s
            outs[1][...] = narrow
            outs[2][...] = narrow[:edge]
            outs[3][...] = narrow[rows - edge :]
        for copy in copies:
            copy.wait()


def load(ids, fronts, width, after):
    rows = fronts.shape[2]
    return pl.pallas_call(
        functools.partial(load_kernel, len(after)),
        in_specs=[
            pl.BlockSpec(memory_space=pltpu.SMEM),
            *[pl.BlockSpec(memory_space=pl.ANY)] * (1 + len(after)),
        ],
        out_specs=pl.BlockSpec(memory_space=pltpu.VMEM),
        out_shape=pltpu.VMEM((2, rows, width), fronts.dtype),
        scratch_shapes=[pltpu.SemaphoreType.DMA((4,))],
        compiler_params=pltpu.CompilerParams(vmem_limit_bytes=VMEM_LIMIT),
        cost_estimate=pl.CostEstimate(
            flops=0, bytes_accessed=4 * rows * width, transcendentals=0
        ),
    )(ids, fronts, *after)


def multiply(ids, xs, fronts, block, acc=None, rhs=None, kept=()):
    _, width, lanes = xs[0].shape
    rows = block.shape[1]
    first, last = acc is None, rhs is not None
    vmem = pl.BlockSpec(memory_space=pltpu.VMEM)
    block = pltpu.with_memory_space_constraint(block, pltpu.VMEM)
    operands = [ids, fronts, block, *xs]
    aliases = {}
    if not first:
        if not last:
            aliases[len(operands)] = 0
        operands.append(acc)
    if last:
        operands += [rhs, *kept]
        aliases = {len(operands) - len(kept) + i: 1 + i for i in range(len(kept))}
        out_shape = [jax.ShapeDtypeStruct((1, rows, lanes), jnp.bfloat16)] + [
            jax.ShapeDtypeStruct(keep.shape, keep.dtype) for keep in kept
        ]
    else:
        out_shape = [
            jax.ShapeDtypeStruct((2, rows, lanes), jnp.float32),
            pltpu.VMEM(block.shape, block.dtype),
        ]
    return pl.pallas_call(
        functools.partial(mul_kernel, first, last),
        in_specs=[
            pl.BlockSpec(memory_space=pltpu.SMEM),
            pl.BlockSpec(memory_space=pl.ANY),
            *[vmem] * (len(operands) - 2),
        ],
        out_specs=[vmem] * len(out_shape),
        out_shape=out_shape,
        scratch_shapes=[
            pltpu.VMEM((2 * width, lanes), jnp.bfloat16),
            pltpu.SemaphoreType.DMA((4,)),
        ],
        input_output_aliases=aliases,
        compiler_params=pltpu.CompilerParams(vmem_limit_bytes=VMEM_LIMIT),
        cost_estimate=pl.CostEstimate(
            flops=16 * rows * width * lanes, bytes_accessed=0, transcendentals=0
        ),
    )(*operands)


def residual_kernel(joins, ids_ref, s_ref, rhs_ref, wave_ref, *refs):
    join_refs, (after_ref, above_ref, below_ref, out_ref) = refs[:joins], refs[joins:]
    row_count, columns = wave_ref.shape
    lanes = s_ref.shape[1]
    half = lanes // 2
    first = ids_ref[0] == 1
    thick = ids_ref[3].astype(jnp.float32)
    far = (ids_ref[2] - 1).astype(jnp.float32) - thick
    diagonal = 6.0 - wave_ref[...].T
    edge = jnp.zeros((1, lanes), jnp.float32)
    for i in range(row_count):
        here = pl.ds(i * columns, columns)
        s = s_ref[here]
        row = (ids_ref[1] + i).astype(jnp.float32)
        border = jnp.maximum(0.0, thick - row) + jnp.maximum(0.0, row - far)
        absorb = jnp.full((columns, 1), 2.0 * border, jnp.float32) / thick
        if i > 0:
            above = s_ref[pl.ds((i - 1) * columns, columns)]
        else:
            above = above_ref[...].astype(jnp.float32)
        if i < row_count - 1:
            below = s_ref[pl.ds((i + 1) * columns, columns)]
        else:
            below = below_ref[...].astype(jnp.float32)
        beside = after_ref[here].astype(jnp.float32) + above + below
        beside = beside + jnp.concatenate([edge, s[:-1]]) + jnp.concatenate([s[1:], edge])
        turned = jnp.concatenate([-s[:, half:], s[:, :half]], axis=1)
        joined = jnp.zeros(s.shape, jnp.float32)
        for join_ref in join_refs:
            joined = joined + join_ref[0, here].astype(jnp.float32)
        joined = jnp.where(first, rhs_ref[here], joined)
        out_ref[here] = joined - (diagonal[:, i : i + 1] * s + absorb * turned - beside)


def local(rhs, fronts, wave_sq, pml_width):
    _, rhs_count, row_count, components, columns = rhs.shape
    panels = lax.axis_size("panel")
    front = lax.axis_size("front")
    panel = lax.axis_index("panel")
    place = lax.axis_index("front").astype(jnp.int32)
    rows = row_count * columns
    lanes = components * rhs_count
    masks = [1 << b for b in reversed(range(front.bit_length() - 1))]

    def exchange(values, mask, source, target):
        pairs = [(source * front + (j ^ mask), target * front + j) for j in range(front)]
        return lax.ppermute(values, ("panel", "front"), pairs)

    def shift_panel(values, by):
        pairs = [
            (p * front + j, (p + by) * front + j)
            for p in range(panels)
            for j in range(front)
            if 0 <= p + by < panels
        ]
        return lax.ppermute(values, ("panel", "front"), pairs)

    def send(values, source, target, mask=0):
        return exchange(values, mask, source, target)

    fronts = pltpu.with_memory_space_constraint(fronts, pltpu.HBM)
    rhs_t = rhs[0].transpose(1, 3, 2, 0).reshape(rows, lanes)
    near = [0, masks[-1], masks[-2], masks[-2] | masks[-1]]
    own = rhs_t.astype(jnp.bfloat16)[None]
    rhs_next = shift_panel(rhs_t, -1)
    narrow = own[0]
    kept = [rhs_t, narrow, narrow[:columns], narrow[rows - columns :]]
    joins = []
    for q in range(panels):
        active = (panel == q).astype(jnp.int32)
        sender = q ^ 1
        if q % 2 == 0:
            own = send(own, max(q - 1, 0), sender)
        held, offsets = [own], [0]
        arrived, arrived_offsets = [], []

        def deliver(parts, part_offsets):
            for part, offset in zip(parts, part_offsets):
                for mask in near:
                    arrived.append(send(part, sender, q, mask))
                    arrived_offsets.append(offset ^ mask)

        fresh, fresh_offsets = held, offsets
        for mask in masks[:-2]:
            deliver(fresh, fresh_offsets)
            fresh = [send(part, sender, sender, mask) for part in held]
            fresh_offsets = [o ^ mask for o in offsets]
            held, offsets = held + fresh, offsets + fresh_offsets
        deliver(fresh, fresh_offsets)
        if q > 0:
            joins.append(arrived[0])

        acc = None
        chunks = [place ^ o for o in arrived_offsets]
        bases = [chunk // 2 * 2 * rows for chunk in chunks[::2]]
        block = None
        for pair in range(len(bases)):
            firsts = [chunk % 2 for chunk in chunks[2 * pair : 2 * pair + 2]]
            following = bases[(pair + 1) % len(bases)]
            ids = jnp.stack([active] + firsts + [following])
            xs = arrived[2 * pair : 2 * pair + 2]
            if pair == 0:
                block = load(jnp.stack([active, bases[0]]), fronts, 2 * rows, fresh)
            if pair + 1 < len(bases):
                acc, block = multiply(ids, xs, fronts, block, acc)
            else:
                own, *kept = multiply(ids, xs, fronts, block, acc, rhs_next, kept)

    s, narrow, top, bottom = kept
    after = shift_panel(narrow, -1)
    above = lax.ppermute(bottom, "front", [(j, j + 1) for j in range(front - 1)])
    below = lax.ppermute(top, "front", [(j + 1, j) for j in range(front - 1)])
    row_ids = [panel == 0, place * row_count, row_count * front, pml_width[0]]
    ids = jnp.stack([jnp.asarray(x, jnp.int32) for x in row_ids])
    vmem = pl.BlockSpec(memory_space=pltpu.VMEM)
    residual = pl.pallas_call(
        functools.partial(residual_kernel, len(joins)),
        in_specs=[pl.BlockSpec(memory_space=pltpu.SMEM), *[vmem] * (6 + len(joins))],
        out_specs=vmem,
        out_shape=jax.ShapeDtypeStruct((rows, lanes), jnp.float32),
        compiler_params=pltpu.CompilerParams(vmem_limit_bytes=VMEM_LIMIT),
        cost_estimate=pl.CostEstimate(
            flops=20 * rows * lanes, bytes_accessed=0, transcendentals=0
        ),
    )(ids, s, rhs_t, wave_sq[0], *joins, after, above, below)

    def back(values):
        values = values.reshape(row_count, columns, components, rhs_count)
        return values.transpose(3, 0, 2, 1)[None]

    return (back(s), back(residual))


def solution(mesh):
    return jax.shard_map(
        local,
        mesh=mesh,
        in_specs=(
            P("panel", None, "front", None, None),
            P("panel", None, "front", None),
            P("panel", "front", None),
            P("panel"),
        ),
        out_specs=(P("panel", None, "front", None, None), P("panel", None, "front", None, None)),
        check_vma=False,
    )
```

```python
import functools

import jax
import jax.numpy as jnp
from jax import lax
from jax.experimental import pallas as pl
from jax.experimental.pallas import tpu as pltpu
from jax.sharding import PartitionSpec as P


VMEM_LIMIT = 5 * 1024 * 1024
AHEAD = 3


def pair_copies(base, front_ref, block_ref, sems):
    _, rows, width = block_ref.shape
    half = rows // 2
    return [
        pltpu.make_async_copy(
            front_ref.at[0, part, pl.ds(begin, half), pl.ds(pl.multiple_of(base, width), width)],
            block_ref.at[part, pl.ds(begin, half)],
            sems.at[2 * part + begin // half],
        )
        for part in range(2)
        for begin in (0, half)
    ]


def load_kernel(extra, ids_ref, front_ref, *refs):
    *block_refs, sems = refs[extra:]

    @pl.when(ids_ref[0] == 1)
    def _():
        copies = []
        for pair, block_ref in enumerate(block_refs):
            copies += pair_copies(ids_ref[1 + pair], front_ref, block_ref, sems.at[pair])
        for copy in copies:
            copy.start()
        for copy in copies:
            copy.wait()


def mul_kernel(first, last, fetch, ids_ref, front_ref, block_ref, *refs):
    *refs, x_all, sems = refs
    x_refs, refs = refs[:2], list(refs[2:])
    acc_in = None if first else refs.pop(0)
    if last:
        rhs_ref, *kept = refs[:5]
        own_ref, *outs = refs[5:]

        @pl.when(ids_ref[0] == 0)
        def _():
            for out, keep in zip(outs, kept):
                out[...] = keep[...]

    @pl.when(ids_ref[0] == 1)
    def _():
        width, lanes = x_refs[0].shape[1:]
        rows = block_ref.shape[1]
        copies = []
        if fetch:
            copies = pair_copies(ids_ref[3], front_ref, refs[1], sems)
        for copy in copies:
            copy.start()
        for k, x_ref in enumerate(x_refs):
            x_all[pl.ds(pl.multiple_of(ids_ref[1 + k] * width, width), width)] = x_ref[0]
        block = block_ref[...].reshape(2 * rows, 2 * width)
        term = jnp.dot(block, x_all[...], preferred_element_type=jnp.float32)
        if not first:
            term = term + acc_in[...].reshape(2 * rows, lanes)
        if not last:
            refs[0][...] = term.reshape(2, rows, lanes)
        else:
            half = lanes // 2
            edge = outs[2].shape[0]
            re, im = term[:rows], term[rows:]
            s = re + jnp.concatenate([-im[:, half:], im[:, :half]], axis=1)
            narrow = s.astype(jnp.bfloat16)
            own_ref[0] = (rhs_ref[...] + s).astype(jnp.bfloat16)
            outs[0][...] = s
            outs[1][...] = narrow
            outs[2][...] = narrow[:edge]
            outs[3][...] = narrow[rows - edge :]
        for copy in copies:
            copy.wait()


def load(active, bases, fronts, width, after):
    ids = jnp.stack([active] + bases)
    rows = fronts.shape[2]
    count = len(bases)
    return pl.pallas_call(
        functools.partial(load_kernel, len(after)),
        in_specs=[
            pl.BlockSpec(memory_space=pltpu.SMEM),
            *[pl.BlockSpec(memory_space=pl.ANY)] * (1 + len(after)),
        ],
        out_specs=[pl.BlockSpec(memory_space=pltpu.VMEM)] * count,
        out_shape=[pltpu.VMEM((2, rows, width), fronts.dtype)] * count,
        scratch_shapes=[pltpu.SemaphoreType.DMA((count, 4))],
        compiler_params=pltpu.CompilerParams(vmem_limit_bytes=VMEM_LIMIT),
        cost_estimate=pl.CostEstimate(
            flops=0, bytes_accessed=4 * rows * width * count, transcendentals=0
        ),
    )(ids, fronts, *after)


def multiply(ids, xs, fronts, block, fetch, acc=None, rhs=None, kept=()):
    _, width, lanes = xs[0].shape
    rows = block.shape[1]
    first, last = acc is None, rhs is not None
    vmem = pl.BlockSpec(memory_space=pltpu.VMEM)
    block = pltpu.with_memory_space_constraint(block, pltpu.VMEM)
    operands = [ids, fronts, block, *xs]
    aliases = {}
    if not first:
        if not last:
            aliases[len(operands)] = 0
        operands.append(acc)
    if last:
        operands += [rhs, *kept]
        aliases = {len(operands) - len(kept) + i: 1 + i for i in range(len(kept))}
        out_shape = [jax.ShapeDtypeStruct((1, rows, lanes), jnp.bfloat16)] + [
            jax.ShapeDtypeStruct(keep.shape, keep.dtype) for keep in kept
        ]
    else:
        out_shape = [jax.ShapeDtypeStruct((2, rows, lanes), jnp.float32)]
        if fetch:
            out_shape.append(pltpu.VMEM(block.shape, block.dtype))
    return pl.pallas_call(
        functools.partial(mul_kernel, first, last, fetch),
        in_specs=[
            pl.BlockSpec(memory_space=pltpu.SMEM),
            pl.BlockSpec(memory_space=pl.ANY),
            *[vmem] * (len(operands) - 2),
        ],
        out_specs=[vmem] * len(out_shape),
        out_shape=out_shape,
        scratch_shapes=[
            pltpu.VMEM((2 * width, lanes), jnp.bfloat16),
            pltpu.SemaphoreType.DMA((4,)),
        ],
        input_output_aliases=aliases,
        compiler_params=pltpu.CompilerParams(vmem_limit_bytes=VMEM_LIMIT),
        cost_estimate=pl.CostEstimate(
            flops=16 * rows * width * lanes, bytes_accessed=0, transcendentals=0
        ),
    )(*operands)


def residual_kernel(joins, ids_ref, s_ref, rhs_ref, wave_ref, *refs):
    join_refs, (after_ref, above_ref, below_ref, out_ref) = refs[:joins], refs[joins:]
    row_count, columns = wave_ref.shape
    lanes = s_ref.shape[1]
    half = lanes // 2
    first = ids_ref[0] == 1
    thick = ids_ref[3].astype(jnp.float32)
    far = (ids_ref[2] - 1).astype(jnp.float32) - thick
    diagonal = 6.0 - wave_ref[...].T
    edge = jnp.zeros((1, lanes), jnp.float32)
    for i in range(row_count):
        here = pl.ds(i * columns, columns)
        s = s_ref[here]
        row = (ids_ref[1] + i).astype(jnp.float32)
        border = jnp.maximum(0.0, thick - row) + jnp.maximum(0.0, row - far)
        absorb = jnp.full((columns, 1), 2.0 * border, jnp.float32) / thick
        if i > 0:
            above = s_ref[pl.ds((i - 1) * columns, columns)]
        else:
            above = above_ref[...].astype(jnp.float32)
        if i < row_count - 1:
            below = s_ref[pl.ds((i + 1) * columns, columns)]
        else:
            below = below_ref[...].astype(jnp.float32)
        beside = after_ref[here].astype(jnp.float32) + above + below
        beside = beside + jnp.concatenate([edge, s[:-1]]) + jnp.concatenate([s[1:], edge])
        turned = jnp.concatenate([-s[:, half:], s[:, :half]], axis=1)
        joined = jnp.zeros(s.shape, jnp.float32)
        for join_ref in join_refs:
            joined = joined + join_ref[0, here].astype(jnp.float32)
        joined = jnp.where(first, rhs_ref[here], joined)
        out_ref[here] = joined - (diagonal[:, i : i + 1] * s + absorb * turned - beside)


def local(rhs, fronts, wave_sq, pml_width):
    _, rhs_count, row_count, components, columns = rhs.shape
    panels = lax.axis_size("panel")
    front = lax.axis_size("front")
    panel = lax.axis_index("panel")
    place = lax.axis_index("front").astype(jnp.int32)
    rows = row_count * columns
    lanes = components * rhs_count
    masks = [1 << b for b in reversed(range(front.bit_length() - 1))]

    def exchange(values, mask, source, target):
        pairs = [(source * front + (j ^ mask), target * front + j) for j in range(front)]
        return lax.ppermute(values, ("panel", "front"), pairs)

    def shift_panel(values, by):
        pairs = [
            (p * front + j, (p + by) * front + j)
            for p in range(panels)
            for j in range(front)
            if 0 <= p + by < panels
        ]
        return lax.ppermute(values, ("panel", "front"), pairs)

    def send(values, source, target, mask=0):
        return exchange(values, mask, source, target)

    fronts = pltpu.with_memory_space_constraint(fronts, pltpu.HBM)
    rhs_t = rhs[0].transpose(1, 3, 2, 0).reshape(rows, lanes)
    near = [0, masks[-1], masks[-2], masks[-2] | masks[-1]]
    own = rhs_t.astype(jnp.bfloat16)[None]
    rhs_next = shift_panel(rhs_t, -1)
    narrow = own[0]
    kept = [rhs_t, narrow, narrow[:columns], narrow[rows - columns :]]
    joins = []
    for q in range(panels):
        active = (panel == q).astype(jnp.int32)
        sender = q ^ 1
        if q % 2 == 0:
            own = send(own, max(q - 1, 0), sender)
        held, offsets = [own], [0]
        arrived, arrived_offsets = [], []

        def deliver(parts, part_offsets):
            for part, offset in zip(parts, part_offsets):
                for mask in near:
                    arrived.append(send(part, sender, q, mask))
                    arrived_offsets.append(offset ^ mask)

        fresh, fresh_offsets = held, offsets
        for mask in masks[:-2]:
            deliver(fresh, fresh_offsets)
            fresh = [send(part, sender, sender, mask) for part in held]
            fresh_offsets = [o ^ mask for o in offsets]
            held, offsets = held + fresh, offsets + fresh_offsets
        deliver(fresh, fresh_offsets)
        if q > 0:
            joins.append(arrived[0])

        acc = None
        chunks = [place ^ o for o in arrived_offsets]
        bases = [chunk // 2 * 2 * rows for chunk in chunks[::2]]
        blocks = list(load(active, bases[:AHEAD], fronts, 2 * rows, fresh))
        for pair in range(len(bases)):
            fetch = AHEAD <= len(blocks) < len(bases) and len(blocks) == pair + AHEAD - 1
            firsts = [chunk % 2 for chunk in chunks[2 * pair : 2 * pair + 2]]
            following = bases[min(len(blocks), len(bases) - 1)]
            ids = jnp.stack([active] + firsts + [following])
            xs = arrived[2 * pair : 2 * pair + 2]
            if pair + 1 < len(bases):
                acc, *more = multiply(ids, xs, fronts, blocks[pair], fetch, acc)
                blocks += more
            else:
                own, *kept = multiply(ids, xs, fronts, blocks[pair], False, acc, rhs_next, kept)

    s, narrow, top, bottom = kept
    after = shift_panel(narrow, -1)
    above = lax.ppermute(bottom, "front", [(j, j + 1) for j in range(front - 1)])
    below = lax.ppermute(top, "front", [(j + 1, j) for j in range(front - 1)])
    row_ids = [panel == 0, place * row_count, row_count * front, pml_width[0]]
    ids = jnp.stack([jnp.asarray(x, jnp.int32) for x in row_ids])
    vmem = pl.BlockSpec(memory_space=pltpu.VMEM)
    residual = pl.pallas_call(
        functools.partial(residual_kernel, len(joins)),
        in_specs=[pl.BlockSpec(memory_space=pltpu.SMEM), *[vmem] * (6 + len(joins))],
        out_specs=vmem,
        out_shape=jax.ShapeDtypeStruct((rows, lanes), jnp.float32),
        compiler_params=pltpu.CompilerParams(vmem_limit_bytes=VMEM_LIMIT),
        cost_estimate=pl.CostEstimate(
            flops=20 * rows * lanes, bytes_accessed=0, transcendentals=0
        ),
    )(ids, s, rhs_t, wave_sq[0], *joins, after, above, below)

    def back(values):
        values = values.reshape(row_count, columns, components, rhs_count)
        return values.transpose(3, 0, 2, 1)[None]

    return (back(s), back(residual))


def solution(mesh):
    return jax.shard_map(
        local,
        mesh=mesh,
        in_specs=(
            P("panel", None, "front", None, None),
            P("panel", None, "front", None),
            P("panel", "front", None),
            P("panel"),
        ),
        out_specs=(P("panel", None, "front", None, None), P("panel", None, "front", None, None)),
        check_vma=False,
    )
```

```python
import functools

import jax
import jax.numpy as jnp
from jax import lax
from jax.experimental import pallas as pl
from jax.experimental.pallas import tpu as pltpu
from jax.sharding import PartitionSpec as P


VMEM_LIMIT = 5 * 1024 * 1024
AHEAD = 4


def pair_copies(base, front_ref, block_ref, sems):
    _, rows, width = block_ref.shape
    half = rows // 2
    return [
        pltpu.make_async_copy(
            front_ref.at[0, part, pl.ds(begin, half), pl.ds(pl.multiple_of(base, width), width)],
            block_ref.at[part, pl.ds(begin, half)],
            sems.at[2 * part + begin // half],
        )
        for part in range(2)
        for begin in (0, half)
    ]


def load_kernel(extra, ids_ref, front_ref, *refs):
    *block_refs, sems = refs[extra:]

    @pl.when(ids_ref[0] == 1)
    def _():
        copies = []
        for pair, block_ref in enumerate(block_refs):
            copies += pair_copies(ids_ref[1 + pair], front_ref, block_ref, sems.at[pair])
        for copy in copies:
            copy.start()
        for copy in copies:
            copy.wait()


def mul_kernel(first, last, fetch, ids_ref, front_ref, block_ref, *refs):
    *refs, x_all, sems = refs
    x_refs, refs = refs[:2], list(refs[2:])
    acc_in = None if first else refs.pop(0)
    if last:
        rhs_ref, *kept = refs[:5]
        own_ref, *outs = refs[5:]

        @pl.when(ids_ref[0] == 0)
        def _():
            for out, keep in zip(outs, kept):
                out[...] = keep[...]

    @pl.when(ids_ref[0] == 1)
    def _():
        width, lanes = x_refs[0].shape[1:]
        rows = block_ref.shape[1]
        copies = []
        if fetch:
            copies = pair_copies(ids_ref[3], front_ref, refs[1], sems)
        for copy in copies:
            copy.start()
        for k, x_ref in enumerate(x_refs):
            x_all[pl.ds(pl.multiple_of(ids_ref[1 + k] * width, width), width)] = x_ref[0]
        block = block_ref[...].reshape(2 * rows, 2 * width)
        term = jnp.dot(block, x_all[...], preferred_element_type=jnp.float32)
        if not first:
            term = term + acc_in[...].reshape(2 * rows, lanes)
        if not last:
            refs[0][...] = term.reshape(2, rows, lanes)
        else:
            half = lanes // 2
            edge = outs[2].shape[0]
            re, im = term[:rows], term[rows:]
            s = re + jnp.concatenate([-im[:, half:], im[:, :half]], axis=1)
            narrow = s.astype(jnp.bfloat16)
            own_ref[0] = (rhs_ref[...] + s).astype(jnp.bfloat16)
            outs[0][...] = s
            outs[1][...] = narrow
            outs[2][...] = narrow[:edge]
            outs[3][...] = narrow[rows - edge :]
        for copy in copies:
            copy.wait()


def load(active, bases, fronts, width, after):
    ids = jnp.stack([active] + bases)
    rows = fronts.shape[2]
    count = len(bases)
    return pl.pallas_call(
        functools.partial(load_kernel, len(after)),
        in_specs=[
            pl.BlockSpec(memory_space=pltpu.SMEM),
            *[pl.BlockSpec(memory_space=pl.ANY)] * (1 + len(after)),
        ],
        out_specs=[pl.BlockSpec(memory_space=pltpu.VMEM)] * count,
        out_shape=[pltpu.VMEM((2, rows, width), fronts.dtype)] * count,
        scratch_shapes=[pltpu.SemaphoreType.DMA((count, 4))],
        compiler_params=pltpu.CompilerParams(vmem_limit_bytes=VMEM_LIMIT),
        cost_estimate=pl.CostEstimate(
            flops=0, bytes_accessed=4 * rows * width * count, transcendentals=0
        ),
    )(ids, fronts, *after)


def multiply(ids, xs, fronts, block, fetch, acc=None, rhs=None, kept=()):
    _, width, lanes = xs[0].shape
    rows = block.shape[1]
    first, last = acc is None, rhs is not None
    vmem = pl.BlockSpec(memory_space=pltpu.VMEM)
    block = pltpu.with_memory_space_constraint(block, pltpu.VMEM)
    operands = [ids, fronts, block, *xs]
    aliases = {}
    if not first:
        if not last:
            aliases[len(operands)] = 0
        operands.append(acc)
    if last:
        operands += [rhs, *kept]
        aliases = {len(operands) - len(kept) + i: 1 + i for i in range(len(kept))}
        out_shape = [jax.ShapeDtypeStruct((1, rows, lanes), jnp.bfloat16)] + [
            jax.ShapeDtypeStruct(keep.shape, keep.dtype) for keep in kept
        ]
    else:
        out_shape = [jax.ShapeDtypeStruct((2, rows, lanes), jnp.float32)]
        if fetch:
            out_shape.append(pltpu.VMEM(block.shape, block.dtype))
    return pl.pallas_call(
        functools.partial(mul_kernel, first, last, fetch),
        in_specs=[
            pl.BlockSpec(memory_space=pltpu.SMEM),
            pl.BlockSpec(memory_space=pl.ANY),
            *[vmem] * (len(operands) - 2),
        ],
        out_specs=[vmem] * len(out_shape),
        out_shape=out_shape,
        scratch_shapes=[
            pltpu.VMEM((2 * width, lanes), jnp.bfloat16),
            pltpu.SemaphoreType.DMA((4,)),
        ],
        input_output_aliases=aliases,
        compiler_params=pltpu.CompilerParams(vmem_limit_bytes=VMEM_LIMIT),
        cost_estimate=pl.CostEstimate(
            flops=16 * rows * width * lanes, bytes_accessed=0, transcendentals=0
        ),
    )(*operands)


def residual_kernel(joins, ids_ref, s_ref, rhs_ref, wave_ref, *refs):
    join_refs, (after_ref, above_ref, below_ref, out_ref) = refs[:joins], refs[joins:]
    row_count, columns = wave_ref.shape
    lanes = s_ref.shape[1]
    half = lanes // 2
    first = ids_ref[0] == 1
    thick = ids_ref[3].astype(jnp.float32)
    far = (ids_ref[2] - 1).astype(jnp.float32) - thick
    diagonal = 6.0 - wave_ref[...].T
    edge = jnp.zeros((1, lanes), jnp.float32)
    for i in range(row_count):
        here = pl.ds(i * columns, columns)
        s = s_ref[here]
        row = (ids_ref[1] + i).astype(jnp.float32)
        border = jnp.maximum(0.0, thick - row) + jnp.maximum(0.0, row - far)
        absorb = jnp.full((columns, 1), 2.0 * border, jnp.float32) / thick
        if i > 0:
            above = s_ref[pl.ds((i - 1) * columns, columns)]
        else:
            above = above_ref[...].astype(jnp.float32)
        if i < row_count - 1:
            below = s_ref[pl.ds((i + 1) * columns, columns)]
        else:
            below = below_ref[...].astype(jnp.float32)
        beside = after_ref[here].astype(jnp.float32) + above + below
        beside = beside + jnp.concatenate([edge, s[:-1]]) + jnp.concatenate([s[1:], edge])
        turned = jnp.concatenate([-s[:, half:], s[:, :half]], axis=1)
        joined = jnp.zeros(s.shape, jnp.float32)
        for join_ref in join_refs:
            joined = joined + join_ref[0, here].astype(jnp.float32)
        joined = jnp.where(first, rhs_ref[here], joined)
        out_ref[here] = joined - (diagonal[:, i : i + 1] * s + absorb * turned - beside)


def local(rhs, fronts, wave_sq, pml_width):
    _, rhs_count, row_count, components, columns = rhs.shape
    panels = lax.axis_size("panel")
    front = lax.axis_size("front")
    panel = lax.axis_index("panel")
    place = lax.axis_index("front").astype(jnp.int32)
    rows = row_count * columns
    lanes = components * rhs_count
    masks = [1 << b for b in reversed(range(front.bit_length() - 1))]

    def exchange(values, mask, source, target):
        pairs = [(source * front + (j ^ mask), target * front + j) for j in range(front)]
        return lax.ppermute(values, ("panel", "front"), pairs)

    def shift_panel(values, by):
        pairs = [
            (p * front + j, (p + by) * front + j)
            for p in range(panels)
            for j in range(front)
            if 0 <= p + by < panels
        ]
        return lax.ppermute(values, ("panel", "front"), pairs)

    def send(values, source, target, mask=0):
        return exchange(values, mask, source, target)

    fronts = pltpu.with_memory_space_constraint(fronts, pltpu.HBM)
    rhs_t = rhs[0].transpose(1, 3, 2, 0).reshape(rows, lanes)
    near = [0, masks[-1], masks[-2], masks[-2] | masks[-1]]
    own = rhs_t.astype(jnp.bfloat16)[None]
    rhs_next = shift_panel(rhs_t, -1)
    narrow = own[0]
    kept = [rhs_t, narrow, narrow[:columns], narrow[rows - columns :]]
    joins = []
    for q in range(panels):
        active = (panel == q).astype(jnp.int32)
        sender = q ^ 1
        if q % 2 == 0:
            own = send(own, max(q - 1, 0), sender)
        held, offsets = [own], [0]
        arrived, arrived_offsets = [], []

        def deliver(parts, part_offsets):
            for part, offset in zip(parts, part_offsets):
                for mask in near:
                    arrived.append(send(part, sender, q, mask))
                    arrived_offsets.append(offset ^ mask)

        fresh, fresh_offsets = held, offsets
        for mask in masks[:-2]:
            deliver(fresh, fresh_offsets)
            fresh = [send(part, sender, sender, mask) for part in held]
            fresh_offsets = [o ^ mask for o in offsets]
            held, offsets = held + fresh, offsets + fresh_offsets
        deliver(fresh, fresh_offsets)
        if q > 0:
            joins.append(arrived[0])

        acc = None
        chunks = [place ^ o for o in arrived_offsets]
        bases = [chunk // 2 * 2 * rows for chunk in chunks[::2]]
        blocks = list(load(active, bases[:AHEAD], fronts, 2 * rows, fresh))
        for pair in range(len(bases)):
            fetch = AHEAD <= len(blocks) < len(bases) and len(blocks) == pair + AHEAD - 1
            firsts = [chunk % 2 for chunk in chunks[2 * pair : 2 * pair + 2]]
            following = bases[min(len(blocks), len(bases) - 1)]
            ids = jnp.stack([active] + firsts + [following])
            xs = arrived[2 * pair : 2 * pair + 2]
            if pair + 1 < len(bases):
                acc, *more = multiply(ids, xs, fronts, blocks[pair], fetch, acc)
                blocks += more
            else:
                own, *kept = multiply(ids, xs, fronts, blocks[pair], False, acc, rhs_next, kept)

    s, narrow, top, bottom = kept
    after = shift_panel(narrow, -1)
    above = lax.ppermute(bottom, "front", [(j, j + 1) for j in range(front - 1)])
    below = lax.ppermute(top, "front", [(j + 1, j) for j in range(front - 1)])
    row_ids = [panel == 0, place * row_count, row_count * front, pml_width[0]]
    ids = jnp.stack([jnp.asarray(x, jnp.int32) for x in row_ids])
    vmem = pl.BlockSpec(memory_space=pltpu.VMEM)
    residual = pl.pallas_call(
        functools.partial(residual_kernel, len(joins)),
        in_specs=[pl.BlockSpec(memory_space=pltpu.SMEM), *[vmem] * (6 + len(joins))],
        out_specs=vmem,
        out_shape=jax.ShapeDtypeStruct((rows, lanes), jnp.float32),
        compiler_params=pltpu.CompilerParams(vmem_limit_bytes=VMEM_LIMIT),
        cost_estimate=pl.CostEstimate(
            flops=20 * rows * lanes, bytes_accessed=0, transcendentals=0
        ),
    )(ids, s, rhs_t, wave_sq[0], *joins, after, above, below)

    def back(values):
        values = values.reshape(row_count, columns, components, rhs_count)
        return values.transpose(3, 0, 2, 1)[None]

    return (back(s), back(residual))


def solution(mesh):
    return jax.shard_map(
        local,
        mesh=mesh,
        in_specs=(
            P("panel", None, "front", None, None),
            P("panel", None, "front", None),
            P("panel", "front", None),
            P("panel"),
        ),
        out_specs=(P("panel", None, "front", None, None), P("panel", None, "front", None, None)),
        check_vma=False,
    )
```
